1024 devices in a mesh: section: 8 (over z_lo), expert: 16 (over y, x), dp: 8 (over z_hi, core).
Axes of the slice: x: 4, y: 4, z: 32 (z_hi: 4, z_lo: 8; z = z_hi * 8 + z_lo), core: 2. Of those that a mesh axis runs over, the one named last changes fastest.
Arguments:
- section_out: bfloat16 [8, 640, 3072], P('section', 'expert'), may hold values from -6 to 6
- routes_fwd: int32 [8, 640, 4], P('section', 'expert'), may hold values from 0 to 15, all different within a row; in each aligned block of 40 rows (0 to 39, 40 to 79, ..., all dimensions but the last counted through in order) at most 13 rows name the same one
- gate_weight: bfloat16 [16, 3072, 5376], P('expert', None, 'dp'), may hold values from -0.109375 to 0.109375
- up_weight: bfloat16 [16, 3072, 5376], P('expert', None, 'dp'), may hold values from -0.109375 to 0.109375
- routes_bwd: int32 [8, 640, 4], P('section', 'expert'), may hold values from 0 to 15, all different within a row; in each aligned block of 40 rows (0 to 39, 40 to 79, ..., all dimensions but the last counted through in order) at most 13 rows name the same one
- saved_gate: bfloat16 [8, 16, 208, 5376], P('section', 'expert', None, 'dp'), may hold values from -8 to 8
- saved_up: bfloat16 [8, 16, 208, 5376], P('section', 'expert', None, 'dp'), may hold values from -6 to 6
- grad_hidden: bfloat16 [8, 16, 208, 5376], P('section', 'expert', None, 'dp'), may hold values from -6 to 6
Outputs:
- hidden_out: bfloat16 [8, 16, 208, 5376], P('section', 'expert', None, 'dp')
- grad_input: bfloat16 [8, 640, 3072], P('section', 'expert', 'dp')
The draws below stay inside these ranges and needn't reach their ends.
Inputs may be any that keep to these rules, and one draw needn't show every extreme that they name: `routes_fwd`: in each aligned block of 40 rows (one token group) of a section, no expert is named by more than 13 rows, a bound that some block reaches. `routes_bwd`: in each aligned block of 40 rows (one token group) of a section, no expert is named by more than 13 rows, a bound that some block reaches.
All inputs are finite; a program needn't handle non-finite values.
Results may differ from the reference program's by a relative error of at most 0.02.
Values may be sent and summed in bfloat16 or wider, within the bound.
A program may use at most 32 MiB of HBM per device.

```python
import math
from functools import partial
import jax
import jax.numpy as jnp
import numpy as np
from jax import lax

D = 3072
FF = 5376
TOP = 4
TOK = 40
SECTIONS = 8
EXPERTS = 16
TOKENS = 640
CAP = 13
SLOTS = 208
N_DP = 8


def steps_of(stream_key, shape, split, low, top_value):
    def one(dim, blocks):
        heights = jax.random.uniform(jax.random.fold_in(jax.random.fold_in(stream_key, 6), dim), (blocks,), jnp.float32, low / len(split), top_value / len(split))
        return jnp.repeat(jnp.exp(heights), shape[dim] // blocks).reshape((-1,) + (1,) * (len(shape) - dim - 1))

    gain = one(*split[0])
    for cut in split[1:]:
        gain = gain * one(*cut)
    return gain


def routed_block(own_key, own, number, rows, number_of, top, reach, slope):
    order = jax.random.permutation(own_key, number_of)
    heavy_load, usual = load_shares(number_of, rows * top, reach, slope, True), load_shares(number_of, rows * top, reach, slope, False)
    places = jnp.arange(number_of)

    def named(sizes, rotation):
        used = int((sizes > 0).sum())
        fixed = max(1, used // 4)
        shifted = fixed + (places - fixed + rotation * (used - fixed)) % max(1, number_of - fixed)
        return jnp.zeros((number_of,), jnp.int32).at[order[jnp.where(places < fixed, places, shifted)]].set(jnp.asarray(sizes, jnp.int32))

    sizes = jnp.where(number % 4 == 0, named(heavy_load, number // 4), named(usual, number - number // 4 - 1))
    mixed = jax.random.permutation(jax.random.fold_in(own, 3), number_of)
    donor, sink = mixed[0:number_of // 2 * 2:2], mixed[1:number_of // 2 * 2:2]
    room = jnp.minimum(sizes[donor] - 1, reach - sizes[sink]) // 2
    room = jnp.where((donor == order[0]) | (sink == order[0]) | (sizes[sink] == 0), 0, jnp.maximum(room, 0))
    shifted = jax.random.randint(jax.random.fold_in(own, 4), (number_of // 2,), 0, 1 << 20) % (room + 1)
    sizes = sizes.at[donor].add(-shifted).at[sink].add(shifted)
    labels = jnp.searchsorted(jnp.cumsum(sizes), jnp.arange(rows * top), side="right").astype(jnp.int32)
    listing = labels.reshape(top, rows).T
    listing = listing[jax.random.permutation(jax.random.fold_in(own, 1), rows)]
    rotation = jax.random.randint(jax.random.fold_in(own, 2), (rows, 1), 0, top)
    return jnp.take_along_axis(listing, (jnp.arange(top)[None, :] + rotation) % top, axis=1)


def load_shares(amount, total, reach, lean, full):
    weights = [(1 << 20) // math.isqrt(grade ** lean) + 1 for grade in range(1, amount + 1)]
    largest = reach if full else min(reach, max(-(-total // amount), total * weights[0] // sum(weights)))
    least = 1 if total - largest >= amount - 1 else 0
    holding, rest = [largest] + [least] * (amount - 1), total - largest - least * (amount - 1)
    while rest > 0:
        movable = [i for i in range(1, amount) if holding[i] < largest] or [i for i in range(1, amount) if holding[i] < reach]
        whole, remaining = sum([weights[i] for i in movable]), rest
        for i in movable:
            addition = min(reach - holding[i], max(1, remaining * weights[i] // whole), rest)
            holding[i] = holding[i] + addition
            rest = rest - addition
    return np.array(holding)


def bell_draw(key, shape, deviation, most, pieces=(), held_as=jnp.bfloat16):
    loudness = steps_of(key, shape, pieces, -0.22, 0.18) if pieces else 1.0
    entries = jax.random.normal(key, shape, jnp.float32) * deviation * loudness
    return jnp.minimum(jnp.maximum(entries, -most), most).astype(held_as)


def setup_inputs(seed: int = 0) -> dict:
    streams_of = jax.random.split(jax.random.key(seed), 9)
    section_out = bell_draw(streams_of[0], (SECTIONS, TOKENS, D), 1.0, 6.0, ((0, 8), (1, 16)))
    routes_fwd_keys = jax.random.split(jax.random.fold_in(streams_of[1], 1), SECTIONS * TOKENS // TOK)
    routes_fwd_turns = jax.random.permutation(jax.random.fold_in(streams_of[1], 3), SECTIONS * TOKENS // TOK)
    routes_fwd = jax.vmap(lambda own, number: routed_block(jax.random.fold_in(streams_of[1], 2), own, number, TOK, EXPERTS, TOP, CAP, 2))(routes_fwd_keys, routes_fwd_turns).reshape((SECTIONS, TOKENS, TOP))
    gate_weight = bell_draw(streams_of[2], (EXPERTS, D, FF), D ** -0.5, 0.109375, ((0, 16), (2, 8)))
    up_weight = bell_draw(streams_of[3], (EXPERTS, D, FF), D ** -0.5, 0.109375, ((0, 16), (2, 8)))
    routes_bwd_keys = jax.random.split(jax.random.fold_in(streams_of[4], 1), SECTIONS * TOKENS // TOK)
    routes_bwd_turns = jax.random.permutation(jax.random.fold_in(streams_of[4], 3), SECTIONS * TOKENS // TOK)
    routes_bwd = jax.vmap(lambda own, number: routed_block(jax.random.fold_in(streams_of[4], 2), own, number, TOK, EXPERTS, TOP, CAP, 2))(routes_bwd_keys, routes_bwd_turns).reshape((SECTIONS, TOKENS, TOP))
    saved_gate = bell_draw(streams_of[5], (SECTIONS, EXPERTS, SLOTS, FF), 1.5, 8.0, ((0, 8), (1, 16), (3, 8)))
    saved_up = bell_draw(streams_of[6], (SECTIONS, EXPERTS, SLOTS, FF), 1.0, 6.0, ((0, 8), (1, 16), (3, 8)))
    grad_hidden = bell_draw(streams_of[7], (SECTIONS, EXPERTS, SLOTS, FF), 1.0, 6.0, ((0, 8), (1, 16), (3, 8)))
    return {"section_out": section_out, "routes_fwd": routes_fwd, "gate_weight": gate_weight, "up_weight": up_weight, "routes_bwd": routes_bwd, "saved_gate": saved_gate, "saved_up": saved_up, "grad_hidden": grad_hidden}


def slot_table(routes_group, experts, capacity):
    tokens_here = routes_group.shape[0]
    chosen = routes_group.reshape(-1).astype(jnp.int32)
    onehot = (chosen[:, None] == jnp.arange(experts, dtype=jnp.int32)[None, :]).astype(jnp.int32)
    earlier = jnp.cumsum(onehot, axis=0) - onehot
    position = jnp.sum(earlier * onehot, axis=1)
    slot_index = (chosen * capacity + position).reshape(tokens_here, -1)
    targets = jnp.arange(experts * capacity, dtype=jnp.int32)
    matches = jnp.sum((slot_index[None, :, :] == targets[:, None, None]).astype(jnp.int32), axis=2)
    return matches.astype(jnp.bfloat16)


def expert_forward(operands):
    routed_rows, gate_w, up_w = operands
    gate_pre = jnp.dot(routed_rows, gate_w, preferred_element_type=jnp.float32)
    up_pre = jnp.dot(routed_rows, up_w, preferred_element_type=jnp.float32)
    return (jax.nn.silu(gate_pre) * up_pre).astype(jnp.bfloat16)


def expert_backward(operands):
    gate_saved, up_saved, grad_h, gate_w, up_w = operands
    gate_pre = gate_saved.astype(jnp.float32)
    up_pre = up_saved.astype(jnp.float32)
    cotangent = grad_h.astype(jnp.float32)
    sigmoid_gate = jax.nn.sigmoid(gate_pre)
    grad_up = (cotangent * gate_pre * sigmoid_gate).astype(jnp.bfloat16)
    grad_gate = (cotangent * up_pre * sigmoid_gate * (1.0 + gate_pre * (1.0 - sigmoid_gate))).astype(jnp.bfloat16)
    width_block = FF // N_DP
    running = jnp.zeros((gate_pre.shape[0], D), jnp.float32)
    for block_index in range(N_DP):
        first_unit = block_index * width_block
        last_unit = first_unit + width_block
        partial_sum = jnp.dot(grad_gate[:, first_unit:last_unit], gate_w[:, first_unit:last_unit].T, preferred_element_type=jnp.float32)
        partial_sum = partial_sum + jnp.dot(grad_up[:, first_unit:last_unit], up_w[:, first_unit:last_unit].T, preferred_element_type=jnp.float32)
        rounded = lax.optimization_barrier(partial_sum.astype(jnp.bfloat16))
        running = running + rounded.astype(jnp.float32)
    return running.astype(jnp.bfloat16)


def one_section(operands, gate_w, up_w):
    tokens_in, fwd_routes, bwd_routes, gate_saved, up_saved, grad_h = operands
    table_fn = jax.vmap(partial(slot_table, experts=EXPERTS, capacity=CAP))
    fwd_maps = table_fn(fwd_routes.reshape(EXPERTS, TOK, TOP))
    grouped = tokens_in.reshape(EXPERTS, TOK, D).astype(jnp.float32)
    dispatched = jnp.einsum("jst,jtd->jsd", fwd_maps.astype(jnp.float32), grouped, precision=lax.Precision.HIGHEST)
    arrived = dispatched.reshape(EXPERTS, EXPERTS, CAP, D).transpose(1, 0, 2, 3).reshape(EXPERTS, SLOTS, D).astype(jnp.bfloat16)
    hidden = lax.map(expert_forward, (arrived, gate_w, up_w))
    row_grads = lax.map(expert_backward, (gate_saved, up_saved, grad_h, gate_w, up_w))
    returned = row_grads.reshape(EXPERTS, EXPERTS, CAP, D).transpose(1, 0, 2, 3).reshape(EXPERTS, SLOTS, D).astype(jnp.float32)
    bwd_maps = table_fn(bwd_routes.reshape(EXPERTS, TOK, TOP))
    token_grads = jnp.einsum("jst,jsd->jtd", bwd_maps.astype(jnp.float32), returned, precision=lax.Precision.HIGHEST)
    return hidden, token_grads.reshape(TOKENS, D).astype(jnp.bfloat16)


def reference(section_out, routes_fwd, gate_weight, up_weight, routes_bwd, saved_gate, saved_up, grad_hidden):
    inbound = jnp.roll(section_out, 1, axis=0)
    section_fn = partial(one_section, gate_w=gate_weight, up_w=up_weight)
    hidden_out, grad_input = lax.map(section_fn, (inbound, routes_fwd, routes_bwd, saved_gate, saved_up, grad_hidden))
    return hidden_out, grad_input
```

```python
import jax
import jax.numpy as jnp
from jax import lax
from jax.experimental import pallas as pl
from jax.experimental.pallas import tpu as pltpu
from jax.sharding import PartitionSpec as P

MESH = pl.DeviceIdType.MESH
F32, BF16 = jnp.float32, jnp.bfloat16

TOK = 40
TOKP = 48
CAP = 13
CAPP = 16
EXPERTS = 16
ROWS = EXPERTS * CAP
ROWSP = EXPERTS * CAPP
D = 3072
HALF = D // 2
BLOCK = D // 8
HI = 4
PIECES = 3
WIDE = HALF // PIECES
FAR_FIRST = (2, 1, 3, 0)


def dot(a, b):
    return jnp.dot(a, b, preferred_element_type=F32)


def dot_t(a, b):
    return lax.dot_general(a, b, (((1,), (1,)), ((), ())), preferred_element_type=F32)


def iota(shape, dim):
    return lax.broadcasted_iota(jnp.int32, shape, dim)


def positions(routes):
    e = iota((EXPERTS, TOK), 0)
    picked = jnp.zeros((EXPERTS, TOK), F32)
    for k in range(routes.shape[0]):
        picked = picked + (routes[k : k + 1, :] == e).astype(F32)
    picked = picked.astype(BF16)
    row, column = iota((TOK, TOKP), 0), iota((TOK, TOKP), 1)
    earlier = dot(picked, (row < column).astype(F32).astype(BF16))
    here = dot(picked, (row == column).astype(F32).astype(BF16))
    return jnp.where(here > 0.5, earlier, 99.0).astype(BF16)


def padding(shape, slot_dim):
    slot, row = iota(shape, slot_dim), iota(shape, 1 - slot_dim)
    return (slot // CAP * CAPP + slot % CAP == row).astype(F32).astype(BF16)


def kernel(
    sec, rf, gw, uw, rb, sg, su, gh,
    hidden_ref, grad_ref,
    secv, rfv, rbv, gwv, uwv, sgv, suv, ghv,
    tsend, trecv, pbuf, xrecv, asend, arecv, zsend, zrecv, fsend, frecv, foth,
    small_sem, load_sem, w_sem, ts, tr, xs, xr, as_, ar, zs, zr, fs, fr, gs, gr,
):
    s, e, d = lax.axis_index("section"), lax.axis_index("expert"), lax.axis_index("dp")
    h, c = lax.div(d, 2), lax.rem(d, 2)
    other = {"section": s, "expert": e, "dp": h * 2 + (1 - c)}

    def along_z(step):
        z = lax.rem(h * 8 + s + step + 32, 32)
        return {"section": lax.rem(z, 8), "expert": e, "dp": lax.div(z, 8) * 2 + c}

    def plane(i):
        y = lax.rem(lax.div(e, 4) + lax.div(i, 4), 4)
        x = lax.rem(lax.rem(e, 4) + lax.rem(i, 4), 4)
        return y * 4 + x

    def hi(step):
        return lax.rem(h + step, HI)

    saved = [pltpu.make_async_copy(a.at[0, 0], v, load_sem.at[i]) for i, (a, v) in enumerate(((sg, sgv), (su, suv), (gh, ghv)))]
    for copy in saved:
        copy.start()
    weights = []
    for k in range(HI):
        rows = pl.ds(pl.multiple_of(hi(FAR_FIRST[k]) * 2 * BLOCK, 2 * BLOCK), 2 * BLOCK)
        pair = [
            pltpu.make_async_copy(gw.at[0, :, rows], gwv.at[:, rows], w_sem.at[k, 0]),
            pltpu.make_async_copy(uw.at[0, :, rows], uwv.at[:, rows], w_sem.at[k, 1]),
        ]
        for copy in pair:
            copy.start()
        weights.append((rows, pair))

    small = [pltpu.make_async_copy(a.at[0], v, small_sem.at[i]) for i, (a, v) in enumerate(((sec, secv), (rf, rfv), (rb, rbv)))]
    for copy in small:
        copy.start()

    barrier = pltpu.get_barrier_semaphore()

    def greet(i, carry):
        pl.semaphore_signal(barrier, inc=1, device_id={"section": s, "expert": plane(i), "dp": d}, device_id_type=MESH)
        return carry

    for k in range(HI - 1):
        pl.semaphore_signal(
            barrier, inc=1, device_id={"section": s, "expert": e, "dp": hi(FAR_FIRST[k]) * 2 + c}, device_id_type=MESH
        )
    pl.semaphore_signal(barrier, inc=1, device_id=along_z(-1), device_id_type=MESH)
    pl.semaphore_signal(barrier, inc=1, device_id=other, device_id_type=MESH)
    lax.fori_loop(1, EXPERTS, greet, 0)

    for copy in small:
        copy.wait()

    tsend[0:TOK, :] = secv[:, pl.ds(pl.multiple_of(c * HALF, HALF), HALF)]
    tsend[TOK:TOKP, :] = jnp.zeros((TOKP - TOK, HALF), BF16)

    spread = (iota((ROWSP, EXPERTS), 0) // CAPP == iota((ROWSP, EXPERTS), 1)).astype(F32).astype(BF16)
    pos_f, pos_b = positions(rfv[...]), positions(rbv[...])
    within = (iota((ROWSP, TOKP), 0) % CAPP).astype(F32)
    map_f = (dot(spread, pos_f) == within).astype(F32).astype(BF16)
    within_t = (iota((TOKP, ROWSP), 1) % CAPP).astype(F32)
    same = (iota((TOKP, TOKP), 0) == iota((TOKP, TOKP), 1)).astype(F32).astype(BF16)
    pos_b = dot_t(same, pos_b).astype(BF16)
    map_b = (dot_t(pos_b, spread) == within_t).astype(F32).astype(BF16)

    for copy in saved:
        copy.wait()
    g, u, ct = sgv[...].astype(F32), suv[...].astype(F32), ghv[...].astype(F32)
    sig = jax.nn.sigmoid(g)
    grad_up = (ct * g * sig).astype(BF16)
    grad_gate = (ct * u * sig * (1.0 + g * (1.0 - sig))).astype(BF16)
    pad = padding((ROWSP, ROWS), 1)
    grad_up = dot(pad, grad_up).astype(BF16)
    grad_gate = dot(pad, grad_gate).astype(BF16)
    for k in range(HI):
        rows, pair = weights[k]
        for copy in pair:
            copy.wait()
        part = dot(grad_gate, gwv[:, rows]) + dot(grad_up, uwv[:, rows])
        pbuf[k, 0] = part[:, :BLOCK].astype(BF16)
        pbuf[k, 1] = part[:, BLOCK:].astype(BF16)

    pl.semaphore_wait(barrier, EXPERTS - 1 + HI - 1 + 2)

    shift = pltpu.make_async_remote_copy(tsend, trecv, ts, tr, device_id=along_z(1), device_id_type=MESH)
    shift.start()
    swaps = []
    for k in range(HI):
        copy = pltpu.make_async_remote_copy(
            pbuf.at[k, 1 - c], xrecv.at[k], xs.at[k], xr.at[k], device_id=other, device_id_type=MESH
        )
        copy.start()
        swaps.append(copy)

    mine = pl.ds(pl.multiple_of(e * CAPP, CAPP), CAPP)
    for k in range(HI):
        swaps[k].wait_recv()
        asend[k] = (pbuf[k, c].astype(F32) + xrecv[k].astype(F32)).astype(BF16)

        def send(i, carry, k=k):
            to = plane(i)
            pltpu.make_async_remote_copy(
                asend.at[k, pl.ds(pl.multiple_of(to * CAPP, CAPP), CAPP)], arecv.at[k, mine], as_.at[k], ar.at[k],
                device_id={"section": s, "expert": to, "dp": d}, device_id_type=MESH,
            ).start()
            return carry

        lax.fori_loop(1, EXPERTS, send, 0)
        arecv[k, mine] = asend[k, mine]

    shift.wait_recv()
    fsend[...] = dot(map_f, trecv[...]).astype(BF16)
    for p in range(PIECES):
        lanes = pl.ds(p * WIDE, WIDE)

        def send_f(i, carry, p=p, lanes=lanes):
            to = plane(i)
            pltpu.make_async_remote_copy(
                fsend.at[pl.ds(pl.multiple_of(to * CAPP, CAPP), CAPP), lanes], frecv.at[mine, lanes], fs.at[p], fr.at[p],
                device_id={"section": s, "expert": to, "dp": d}, device_id_type=MESH,
            ).start()
            return carry

        lax.fori_loop(1, EXPERTS, send_f, 0)
    frecv[mine, :] = fsend[mine, :]

    most = pl.ds(0, ROWSP - CAPP)
    out_z = []
    own = None
    for k in range(HI):
        pltpu.make_async_copy(asend.at[k, most], arecv.at[k, most], ar.at[k]).wait()
        total = dot(map_b, arecv[k])
        if k == HI - 1:
            own = total.astype(BF16).astype(F32)
            continue
        zsend[k] = total.astype(BF16)
        copy = pltpu.make_async_remote_copy(
            zsend.at[k], zrecv.at[k], zs.at[k], zr.at[k],
            device_id={"section": s, "expert": e, "dp": hi(FAR_FIRST[k]) * 2 + c}, device_id_type=MESH,
        )
        copy.start()
        out_z.append(copy)

    swaps_f = []
    for p in range(PIECES):
        lanes = pl.ds(p * WIDE, WIDE)
        pltpu.make_async_copy(fsend.at[most, lanes], frecv.at[most, lanes], fr.at[p]).wait()
        copy = pltpu.make_async_remote_copy(
            frecv.at[:, lanes], foth.at[:, lanes], gs.at[p], gr.at[p], device_id=other, device_id_type=MESH
        )
        copy.start()
        swaps_f.append(copy)
    near = pl.ds(pl.multiple_of(c * HALF, HALF), HALF)
    far = pl.ds(pl.multiple_of((1 - c) * HALF, HALF), HALF)
    gate = dot_t(frecv[...], gwv[:, near])
    up = dot_t(frecv[...], uwv[:, near])
    for copy in swaps_f:
        copy.wait_recv()
    gate = gate + dot_t(foth[...], gwv[:, far])
    up = up + dot_t(foth[...], uwv[:, far])
    hidden = (gate * jax.nn.sigmoid(gate) * up).astype(BF16)
    hidden_ref[0, 0] = dot(padding((ROWS, ROWSP), 0), hidden).astype(BF16)

    total = own
    for copy in out_z:
        copy.wait_recv()
    for k in range(HI - 1):
        total = total + zrecv[k].astype(F32)
    grad_ref[0] = total[0:TOK].astype(BF16)

    shift.wait_send()
    for copy in (*swaps, *out_z, *swaps_f):
        copy.wait_send()
    for k in range(HI):
        pltpu.make_async_copy(asend.at[k, most], arecv.at[k, most], as_.at[k]).wait()
    for p in range(PIECES):
        lanes = pl.ds(p * WIDE, WIDE)
        pltpu.make_async_copy(fsend.at[most, lanes], frecv.at[most, lanes], fs.at[p]).wait()


def turned(a):
    return jnp.swapaxes(a, 1, 2)


def per_device(section_out, routes_fwd, gate_weight, up_weight, routes_bwd, saved_gate, saved_up, grad_hidden):
    width = gate_weight.shape[2]
    hbm, vmem = pl.BlockSpec(memory_space=pltpu.HBM), pl.BlockSpec(memory_space=pltpu.VMEM)
    dma = pltpu.SemaphoreType.DMA
    return pl.pallas_call(
        kernel,
        out_shape=(
            jax.ShapeDtypeStruct((1, 1, ROWS, width), BF16),
            jax.ShapeDtypeStruct((1, TOK, BLOCK), BF16),
        ),
        in_specs=[hbm] * 8,
        out_specs=(vmem, vmem),
        scratch_shapes=[
            pltpu.VMEM((TOK, D), BF16),
            pltpu.VMEM(routes_fwd.shape[:0:-1], jnp.int32),
            pltpu.VMEM(routes_bwd.shape[:0:-1], jnp.int32),
            pltpu.VMEM((width, D), BF16),
            pltpu.VMEM((width, D), BF16),
            pltpu.VMEM((ROWS, width), BF16),
            pltpu.VMEM((ROWS, width), BF16),
            pltpu.VMEM((ROWS, width), BF16),
            pltpu.VMEM((TOKP, HALF), BF16),
            pltpu.VMEM((TOKP, HALF), BF16),
            pltpu.VMEM((HI, 2, ROWSP, BLOCK), BF16),
            pltpu.VMEM((HI, ROWSP, BLOCK), BF16),
            pltpu.VMEM((HI, ROWSP, BLOCK), BF16),
            pltpu.VMEM((HI, ROWSP, BLOCK), BF16),
            pltpu.VMEM((HI - 1, TOKP, BLOCK), BF16),
            pltpu.VMEM((HI - 1, TOKP, BLOCK), BF16),
            pltpu.VMEM((ROWSP, HALF), BF16),
            pltpu.VMEM((ROWSP, HALF), BF16),
            pltpu.VMEM((ROWSP, HALF), BF16),
            dma((3,)), dma((3,)), dma((HI, 2)), dma, dma, dma((HI,)), dma((HI,)), dma((HI,)), dma((HI,)),
            dma((HI - 1,)), dma((HI - 1,)), dma((PIECES,)), dma((PIECES,)), dma((PIECES,)), dma((PIECES,)),
        ],
        compiler_params=pltpu.CompilerParams(
            collective_id=0, has_side_effects=True, vmem_limit_bytes=60 * 1024 * 1024
        ),
    )(section_out, turned(routes_fwd), turned(gate_weight), turned(up_weight), turned(routes_bwd), saved_gate, saved_up, grad_hidden)


def solution(mesh):
    in_specs = (
        P("section", "expert", None),
        P("section", "expert", None),
        P("expert", None, "dp"),
        P("expert", None, "dp"),
        P("section", "expert", None),
        P("section", "expert", None, "dp"),
        P("section", "expert", None, "dp"),
        P("section", "expert", None, "dp"),
    )
    out_specs = (P("section", "expert", None, "dp"), P("section", "expert", "dp"))
    return jax.shard_map(
        per_device, mesh=mesh, in_specs=in_specs, out_specs=out_specs, check_vma=False
    )
```

```python
import jax
import jax.numpy as jnp
from jax import lax
from jax.experimental import pallas as pl
from jax.experimental.pallas import tpu as pltpu
from jax.sharding import PartitionSpec as P

MESH = pl.DeviceIdType.MESH
F32, BF16 = jnp.float32, jnp.bfloat16

TOK = 40
TOKP = 48
CAP = 13
CAPP = 16
EXPERTS = 16
ROWS = EXPERTS * CAP
ROWSP = EXPERTS * CAPP
D = 3072
HALF = D // 2
BLOCK = D // 8
HI = 4
PIECES = 3
WIDE = HALF // PIECES
FAR_FIRST = (2, 1, 3, 0)


def dot(a, b):
    return jnp.dot(a, b, preferred_element_type=F32)


def dot_t(a, b):
    return lax.dot_general(a, b, (((1,), (1,)), ((), ())), preferred_element_type=F32)


def iota(shape, dim):
    return lax.broadcasted_iota(jnp.int32, shape, dim)


def positions(routes):
    e = iota((EXPERTS, TOK), 0)
    picked = jnp.zeros((EXPERTS, TOK), F32)
    for k in range(routes.shape[0]):
        picked = picked + (routes[k : k + 1, :] == e).astype(F32)
    picked = picked.astype(BF16)
    row, column = iota((TOK, TOKP), 0), iota((TOK, TOKP), 1)
    earlier = dot(picked, (row < column).astype(F32).astype(BF16))
    here = dot(picked, (row == column).astype(F32).astype(BF16))
    return jnp.where(here > 0.5, earlier, 99.0).astype(BF16)


def padding(shape, slot_dim):
    slot, row = iota(shape, slot_dim), iota(shape, 1 - slot_dim)
    return (slot // CAP * CAPP + slot % CAP == row).astype(F32).astype(BF16)


def kernel(
    sec, rf, gw, uw, rb, sg, su, gh,
    hidden_ref, zrecv,
    hidv, secv, rfv, rbv, gwv, uwv, sgv, suv, ghv,
    tsend, trecv, pbuf, xrecv, asend, arecv, zsend, fsend, frecv, foth,
    out_sem, small_sem, load_sem, w_sem, ts, tr, xs, xr, as_, ar, zs, zr, fs, fr, gs, gr, ready,
):
    s, e, d = lax.axis_index("section"), lax.axis_index("expert"), lax.axis_index("dp")
    h, c = lax.div(d, 2), lax.rem(d, 2)
    other = {"section": s, "expert": e, "dp": h * 2 + (1 - c)}

    def along_z(step):
        z = lax.rem(h * 8 + s + step + 32, 32)
        return {"section": lax.rem(z, 8), "expert": e, "dp": lax.div(z, 8) * 2 + c}

    def plane(i):
        y = lax.rem(lax.div(e, 4) + lax.div(i, 4), 4)
        x = lax.rem(lax.rem(e, 4) + lax.rem(i, 4), 4)
        return y * 4 + x

    def hi(step):
        return lax.rem(h + step, HI)

    saved = [pltpu.make_async_copy(a.at[0, 0], v, load_sem.at[i]) for i, (a, v) in enumerate(((sg, sgv), (su, suv), (gh, ghv)))]
    for copy in saved:
        copy.start()
    weights = []
    for k in range(HI):
        rows = pl.ds(pl.multiple_of(hi(FAR_FIRST[k]) * 2 * BLOCK, 2 * BLOCK), 2 * BLOCK)
        pair = [
            pltpu.make_async_copy(gw.at[0, :, rows], gwv.at[:, rows], w_sem.at[k, 0]),
            pltpu.make_async_copy(uw.at[0, :, rows], uwv.at[:, rows], w_sem.at[k, 1]),
        ]
        for copy in pair:
            copy.start()
        weights.append((rows, pair))

    small = [pltpu.make_async_copy(a.at[0], v, small_sem.at[i]) for i, (a, v) in enumerate(((sec, secv), (rf, rfv), (rb, rbv)))]
    for copy in small:
        copy.start()

    barrier = pltpu.get_barrier_semaphore()

    def greet(i, carry):
        pl.semaphore_signal(barrier, inc=1, device_id={"section": s, "expert": plane(i), "dp": d}, device_id_type=MESH)
        return carry

    for r in range(1, HI):

        @pl.when(r > h)
        def _(r=r):
            pl.semaphore_signal(barrier, inc=1, device_id={"section": s, "expert": e, "dp": r * 2 + c}, device_id_type=MESH)

    pl.semaphore_signal(barrier, inc=1, device_id=along_z(-1), device_id_type=MESH)
    pl.semaphore_signal(barrier, inc=1, device_id=other, device_id_type=MESH)
    lax.fori_loop(1, EXPERTS, greet, 0)

    for copy in small:
        copy.wait()

    tsend[0:TOK, :] = secv[:, pl.ds(pl.multiple_of(c * HALF, HALF), HALF)]
    tsend[TOK:TOKP, :] = jnp.zeros((TOKP - TOK, HALF), BF16)

    for copy in saved:
        copy.wait()
    g, u, ct = sgv[...].astype(F32), suv[...].astype(F32), ghv[...].astype(F32)
    sig = jax.nn.sigmoid(g)
    grad_up = (ct * g * sig).astype(BF16)
    grad_gate = (ct * u * sig * (1.0 + g * (1.0 - sig))).astype(BF16)
    pad = padding((ROWSP, ROWS), 1)
    grad_up = dot(pad, grad_up).astype(BF16)
    grad_gate = dot(pad, grad_gate).astype(BF16)
    mine = pl.ds(pl.multiple_of(e * CAPP, CAPP), CAPP)
    swaps = []

    def partial(k):
        rows, pair = weights[k]
        for copy in pair:
            copy.wait()
        part = dot(grad_gate, gwv[:, rows]) + dot(grad_up, uwv[:, rows])
        pbuf[k, 0] = part[:, :BLOCK].astype(BF16)
        pbuf[k, 1] = part[:, BLOCK:].astype(BF16)

    def swap(k):
        copy = pltpu.make_async_remote_copy(
            pbuf.at[k, 1 - c], xrecv.at[k], xs.at[k], xr.at[k], device_id=other, device_id_type=MESH
        )
        copy.start()
        swaps.append(copy)

    def spread_out(k):
        swaps[k].wait_recv()
        asend[k] = (pbuf[k, c].astype(F32) + xrecv[k].astype(F32)).astype(BF16)

        def send(i, carry):
            to = plane(i)
            pltpu.make_async_remote_copy(
                asend.at[k, pl.ds(pl.multiple_of(to * CAPP, CAPP), CAPP)], arecv.at[k, mine], as_.at[k], ar.at[k],
                device_id={"section": s, "expert": to, "dp": d}, device_id_type=MESH,
            ).start()
            return carry

        lax.fori_loop(1, EXPERTS, send, 0)
        arecv[k, mine] = asend[k, mine]

    partial(0)
    pl.semaphore_wait(barrier, EXPERTS - 1 + 2 + h)
    shift = pltpu.make_async_remote_copy(tsend, trecv, ts, tr, device_id=along_z(1), device_id_type=MESH)
    shift.start()
    swap(0)
    for r in range(HI - 1):

        @pl.when(r < h)
        def _(r=r):
            pl.semaphore_signal(ready, inc=1, device_id={"section": s, "expert": e, "dp": r * 2 + c}, device_id_type=MESH)

    partial(1)
    swap(1)
    partial(2)
    swap(2)
    spread_out(0)
    partial(3)
    swap(3)
    for k in range(1, HI):
        spread_out(k)

    spread = (iota((ROWSP, EXPERTS), 0) // CAPP == iota((ROWSP, EXPERTS), 1)).astype(F32).astype(BF16)
    pos_f, pos_b = positions(rfv[...]), positions(rbv[...])
    within = (iota((ROWSP, TOKP), 0) % CAPP).astype(F32)
    map_f = (dot(spread, pos_f) == within).astype(F32).astype(BF16)
    within_t = (iota((TOKP, ROWSP), 1) % CAPP).astype(F32)
    same = (iota((TOKP, TOKP), 0) == iota((TOKP, TOKP), 1)).astype(F32).astype(BF16)
    pos_b = dot_t(same, pos_b).astype(BF16)
    map_b = (dot_t(pos_b, spread) == within_t).astype(F32).astype(BF16)

    most = pl.ds(0, ROWSP - CAPP)
    out_z = [
        pltpu.make_async_remote_copy(
            zsend.at[k], zrecv.at[k], zs.at[k], zr.at[k],
            device_id={"section": s, "expert": e, "dp": hi(FAR_FIRST[k]) * 2 + c}, device_id_type=MESH,
        )
        for k in range(HI - 1)
    ]

    def combine(k):
        pltpu.make_async_copy(asend.at[k, most], arecv.at[k, most], ar.at[k]).wait()
        zsend[k] = dot(map_b, arecv[k]).astype(BF16)

    @pl.when(h == HI - 2)
    def _():
        pl.semaphore_wait(ready, 1)

    @pl.when(h >= 2)
    def _():
        for k in range(HI - 1):
            combine(k)
            out_z[k].start()

    @pl.when(h < 2)
    def _():
        for k in range(HI - 1):
            combine(k)

    combine(HI - 1)

    shift.wait_recv()
    fsend[...] = dot(map_f, trecv[...]).astype(BF16)
    for p in range(PIECES):
        lanes = pl.ds(p * WIDE, WIDE)

        def send_f(i, carry, p=p, lanes=lanes):
            to = plane(i)
            pltpu.make_async_remote_copy(
                fsend.at[pl.ds(pl.multiple_of(to * CAPP, CAPP), CAPP), lanes], frecv.at[mine, lanes], fs.at[p], fr.at[p],
                device_id={"section": s, "expert": to, "dp": d}, device_id_type=MESH,
            ).start()
            return carry

        lax.fori_loop(1, EXPERTS, send_f, 0)
    frecv[mine, :] = fsend[mine, :]

    @pl.when(h < 2)
    def _():
        pl.semaphore_wait(ready, HI - 1 - h)
        for k in range(HI - 1):
            out_z[k].start()

    swaps_f = []
    for p in range(PIECES):
        lanes = pl.ds(p * WIDE, WIDE)
        pltpu.make_async_copy(fsend.at[most, lanes], frecv.at[most, lanes], fr.at[p]).wait()
        copy = pltpu.make_async_remote_copy(
            frecv.at[:, lanes], foth.at[:, lanes], gs.at[p], gr.at[p], device_id=other, device_id_type=MESH
        )
        copy.start()
        swaps_f.append(copy)
    near = pl.ds(pl.multiple_of(c * HALF, HALF), HALF)
    far = pl.ds(pl.multiple_of((1 - c) * HALF, HALF), HALF)
    gate = dot_t(frecv[...], gwv[:, near])
    up = dot_t(frecv[...], uwv[:, near])
    for copy in swaps_f:
        copy.wait_recv()
    gate = gate + dot_t(foth[...], gwv[:, far])
    up = up + dot_t(foth[...], uwv[:, far])
    hidden = (gate * jax.nn.sigmoid(gate) * up).astype(BF16)
    hidv[...] = dot(padding((ROWS, ROWSP), 0), hidden).astype(BF16)
    keep = [
        pltpu.make_async_copy(hidv, hidden_ref, out_sem.at[0]),
        pltpu.make_async_copy(zsend.at[HI - 1], zrecv.at[HI - 1], out_sem.at[1]),
    ]
    for copy in keep:
        copy.start()

    for copy in keep:
        copy.wait()
    for copy in out_z:
        copy.wait_recv()
    shift.wait_send()
    for copy in (*swaps, *out_z, *swaps_f):
        copy.wait_send()
    for k in range(HI):
        pltpu.make_async_copy(asend.at[k, most], arecv.at[k, most], as_.at[k]).wait()
    for p in range(PIECES):
        lanes = pl.ds(p * WIDE, WIDE)
        pltpu.make_async_copy(fsend.at[most, lanes], frecv.at[most, lanes], fs.at[p]).wait()


def finish(hidden, blocks, hidden_out, grad_out, hidv, blocksv, gradv, sem):
    fetch = pltpu.make_async_copy(blocks, blocksv, sem.at[0])
    fetch.start()
    bring = pltpu.make_async_copy(hidden, hidv, sem.at[1])
    bring.start()
    fetch.wait()
    total = blocksv[0].astype(F32)
    for k in range(1, HI):
        total = total + blocksv[k].astype(F32)
    gradv[...] = total[0:TOK].astype(BF16)
    out = pltpu.make_async_copy(gradv, grad_out.at[0], sem.at[2])
    out.start()
    bring.wait()
    put = pltpu.make_async_copy(hidv, hidden_out.at[0, 0], sem.at[3])
    put.start()
    out.wait()
    put.wait()


def turned(a):
    return jnp.swapaxes(a, 1, 2)


def per_device(section_out, routes_fwd, gate_weight, up_weight, routes_bwd, saved_gate, saved_up, grad_hidden):
    width = gate_weight.shape[2]
    hbm = pl.BlockSpec(memory_space=pltpu.HBM)
    dma = pltpu.SemaphoreType.DMA
    hidden, blocks = pl.pallas_call(
        kernel,
        out_shape=(
            jax.ShapeDtypeStruct((ROWS, width), BF16),
            jax.ShapeDtypeStruct((HI, TOKP, BLOCK), BF16),
        ),
        in_specs=[hbm] * 8,
        out_specs=(hbm, hbm),
        scratch_shapes=[
            pltpu.VMEM((ROWS, width), BF16),
            pltpu.VMEM((TOK, D), BF16),
            pltpu.VMEM(routes_fwd.shape[:0:-1], jnp.int32),
            pltpu.VMEM(routes_bwd.shape[:0:-1], jnp.int32),
            pltpu.VMEM((width, D), BF16),
            pltpu.VMEM((width, D), BF16),
            pltpu.VMEM((ROWS, width), BF16),
            pltpu.VMEM((ROWS, width), BF16),
            pltpu.VMEM((ROWS, width), BF16),
            pltpu.VMEM((TOKP, HALF), BF16),
            pltpu.VMEM((TOKP, HALF), BF16),
            pltpu.VMEM((HI, 2, ROWSP, BLOCK), BF16),
            pltpu.VMEM((HI, ROWSP, BLOCK), BF16),
            pltpu.VMEM((HI, ROWSP, BLOCK), BF16),
            pltpu.VMEM((HI, ROWSP, BLOCK), BF16),
            pltpu.VMEM((HI, TOKP, BLOCK), BF16),
            pltpu.VMEM((ROWSP, HALF), BF16),
            pltpu.VMEM((ROWSP, HALF), BF16),
            pltpu.VMEM((ROWSP, HALF), BF16),
            dma((2,)), dma((3,)), dma((3,)), dma((HI, 2)), dma, dma, dma((HI,)), dma((HI,)), dma((HI,)), dma((HI,)),
            dma((HI - 1,)), dma((HI - 1,)), dma((PIECES,)), dma((PIECES,)), dma((PIECES,)), dma((PIECES,)),
            pltpu.SemaphoreType.REGULAR,
        ],
        compiler_params=pltpu.CompilerParams(
            collective_id=0, has_side_effects=True, vmem_limit_bytes=60 * 1024 * 1024
        ),
    )(section_out, turned(routes_fwd), turned(gate_weight), turned(up_weight), turned(routes_bwd), saved_gate, saved_up, grad_hidden)
    return pl.pallas_call(
        finish,
        out_shape=(
            jax.ShapeDtypeStruct((1, 1, ROWS, width), BF16),
            jax.ShapeDtypeStruct((1, TOK, BLOCK), BF16),
        ),
        in_specs=[hbm, hbm],
        out_specs=(hbm, hbm),
        scratch_shapes=[
            pltpu.VMEM((ROWS, width), BF16),
            pltpu.VMEM((HI, TOKP, BLOCK), BF16),
            pltpu.VMEM((TOK, BLOCK), BF16),
            dma((4,)),
        ],
        compiler_params=pltpu.CompilerParams(vmem_limit_bytes=60 * 1024 * 1024),
    )(hidden, blocks)


def solution(mesh):
    in_specs = (
        P("section", "expert", None),
        P("section", "expert", None),
        P("expert", None, "dp"),
        P("expert", None, "dp"),
        P("section", "expert", None),
        P("section", "expert", None, "dp"),
        P("section", "expert", None, "dp"),
        P("section", "expert", None, "dp"),
    )
    out_specs = (P("section", "expert", None, "dp"), P("section", "expert", "dp"))
    return jax.shard_map(
        per_device, mesh=mesh, in_specs=in_specs, out_specs=out_specs, check_vma=False
    )
```

```python
import jax
import jax.numpy as jnp
from jax import lax
from jax.experimental import pallas as pl
from jax.experimental.pallas import tpu as pltpu
from jax.sharding import PartitionSpec as P

MESH = pl.DeviceIdType.MESH
F32, BF16 = jnp.float32, jnp.bfloat16

TOK = 40
TOKP = 48
CAP = 13
CAPP = 16
EXPERTS = 16
ROWS = EXPERTS * CAP
ROWSP = EXPERTS * CAPP
D = 3072
HALF = D // 2
BLOCK = D // 8
LANES = 128
TILES = BLOCK // LANES
PACK = 128
HI = 4
PIECES = 3
WIDE = HALF // PIECES
FAR_FIRST = (2, 1, 3, 0)


def dot(a, b):
    return jnp.dot(a, b, preferred_element_type=F32)


def dot_t(a, b):
    return lax.dot_general(a, b, (((1,), (1,)), ((), ())), preferred_element_type=F32)


def iota(shape, dim):
    return lax.broadcasted_iota(jnp.int32, shape, dim)


def positions(routes):
    e = iota((EXPERTS, TOK), 0)
    picked = jnp.zeros((EXPERTS, TOK), F32)
    for k in range(routes.shape[0]):
        picked = picked + (routes[k : k + 1, :] == e).astype(F32)
    picked = picked.astype(BF16)
    row, column = iota((TOK, TOKP), 0), iota((TOK, TOKP), 1)
    earlier = dot(picked, (row < column).astype(F32).astype(BF16))
    here = dot(picked, (row == column).astype(F32).astype(BF16))
    return jnp.where(here > 0.5, earlier, 99.0).astype(BF16)


def padding(shape, slot_dim):
    slot, row = iota(shape, slot_dim), iota(shape, 1 - slot_dim)
    return (slot // CAP * CAPP + slot % CAP == row).astype(F32).astype(BF16)


def kernel(
    sec, rf, gw, uw, rb, sg, su, gh,
    hidden_ref, zrecv,
    hidv, secv, rfv, rbv, gwv, uwv, sgv, suv, ghv,
    tsend, trecv, pbuf, xrecv, asend, arecv, zsend, fsend, frecv, foth,
    out_sem, small_sem, load_sem, w_sem, ts, tr, xs, xr, as_, ar, zs, zr, fs, fr, gs, gr, ready, follows,
):
    s, e, d = lax.axis_index("section"), lax.axis_index("expert"), lax.axis_index("dp")
    h, c = lax.div(d, 2), lax.rem(d, 2)
    other = {"section": s, "expert": e, "dp": h * 2 + (1 - c)}

    def along_z(step):
        z = lax.rem(h * 8 + s + step + 32, 32)
        return {"section": lax.rem(z, 8), "expert": e, "dp": lax.div(z, 8) * 2 + c}

    def plane(i):
        y = lax.rem(lax.div(e, 4) + lax.div(i, 4), 4)
        x = lax.rem(lax.rem(e, 4) + lax.rem(i, 4), 4)
        return y * 4 + x

    def hi(step):
        return lax.rem(h + step, HI)

    def rank(plane_hi):
        return plane_hi + lax.div(plane_hi, 2) * (5 - 2 * plane_hi)

    saved = [pltpu.make_async_copy(a.at[0, 0], v, load_sem.at[i]) for i, (a, v) in enumerate(((sg, sgv), (su, suv), (gh, ghv)))]
    for copy in saved:
        copy.start()
    weights = []
    for k in range(HI):
        rows = pl.ds(pl.multiple_of(hi(FAR_FIRST[k]) * 2 * BLOCK, 2 * BLOCK), 2 * BLOCK)
        pair = [
            pltpu.make_async_copy(gw.at[0, :, rows], gwv.at[:, rows], w_sem.at[k, 0]),
            pltpu.make_async_copy(uw.at[0, :, rows], uwv.at[:, rows], w_sem.at[k, 1]),
        ]
        for copy in pair:
            copy.start()
        weights.append((rows, pair))

    small = [pltpu.make_async_copy(a.at[0], v, small_sem.at[i]) for i, (a, v) in enumerate(((sec, secv), (rf, rfv), (rb, rbv)))]
    for copy in small:
        copy.start()

    barrier = pltpu.get_barrier_semaphore()

    def greet(i, carry):
        pl.semaphore_signal(barrier, inc=1, device_id={"section": s, "expert": plane(i), "dp": d}, device_id_type=MESH)
        return carry

    for step in range(1, HI):

        @pl.when(rank(hi(step)) > rank(h))
        def _(step=step):
            to = {"section": s, "expert": e, "dp": hi(step) * 2 + c}
            pl.semaphore_signal(barrier, inc=1, device_id=to, device_id_type=MESH)

    place = h * 8 + s
    is_last, is_first = lax.div(place, 31), lax.div(31 - place, 31)

    @pl.when(is_first == 0)
    def _():
        pl.semaphore_signal(barrier, inc=1, device_id=along_z(-1), device_id_type=MESH)

    @pl.when(is_last == 1)
    def _():
        pl.semaphore_signal(barrier, inc=1, device_id=along_z(1), device_id_type=MESH)

    pl.semaphore_signal(barrier, inc=1, device_id=other, device_id_type=MESH)
    lax.fori_loop(1, EXPERTS, greet, 0)

    for copy in small:
        copy.wait()

    tsend[0:TOK, :] = secv[:, pl.ds(pl.multiple_of(c * HALF, HALF), HALF)]
    tsend[TOK:TOKP, :] = jnp.zeros((TOKP - TOK, HALF), BF16)

    shift = pltpu.make_async_remote_copy(tsend, trecv, ts, tr, device_id=along_z(1), device_id_type=MESH)

    def enter():
        pl.semaphore_wait(barrier, EXPERTS - 1 + 2 + rank(h) - is_last + is_first)

        @pl.when(is_last == 0)
        def _():
            shift.start()

        @pl.when(is_first == 1)
        def _():
            pl.semaphore_signal(follows, inc=1, device_id=along_z(-1), device_id_type=MESH)

        for k in range(HI - 1):
            lower = hi(HI - FAR_FIRST[k])

            @pl.when(rank(lower) < rank(h))
            def _(k=k, lower=lower):
                to = {"section": s, "expert": e, "dp": lower * 2 + c}
                pl.semaphore_signal(ready.at[k], inc=1, device_id=to, device_id_type=MESH)

    enters_late = lax.div(rank(h), HI - 1) + is_last + is_first

    @pl.when(enters_late == 0)
    def _():
        enter()

    @pl.when(is_last == 1)
    def _():
        pl.semaphore_wait(follows, 1)
        shift.start()

    for copy in saved:
        copy.wait()
    g, u, ct = sgv[...].astype(F32), suv[...].astype(F32), ghv[...].astype(F32)
    sig = jax.nn.sigmoid(g)
    grad_up = (ct * g * sig).astype(BF16)
    grad_gate = (ct * u * sig * (1.0 + g * (1.0 - sig))).astype(BF16)
    pad = padding((ROWSP, ROWS), 1)
    grad_up = dot(pad, grad_up).astype(BF16)
    grad_gate = dot(pad, grad_gate).astype(BF16)
    mine = pl.ds(pl.multiple_of(e * CAPP, CAPP), CAPP)
    swaps = []

    def partial(k):
        rows, pair = weights[k]
        for copy in pair:
            copy.wait()
        part = dot(grad_gate, gwv[:, rows]) + dot(grad_up, uwv[:, rows])
        pbuf[k, 0] = part[:, :BLOCK].astype(BF16)
        pbuf[k, 1] = part[:, BLOCK:].astype(BF16)

    def swap(k):
        copy = pltpu.make_async_remote_copy(
            pbuf.at[k, 1 - c], xrecv.at[k], xs.at[k], xr.at[k], device_id=other, device_id_type=MESH
        )
        copy.start()
        swaps.append(copy)

    def spread_out(k):
        swaps[k].wait_recv()
        asend[k] = (pbuf[k, c].astype(F32) + xrecv[k].astype(F32)).astype(BF16)

        def send(i, carry):
            to = plane(i)
            pltpu.make_async_remote_copy(
                asend.at[k, pl.ds(pl.multiple_of(to * CAPP, CAPP), CAPP)], arecv.at[k, mine], as_.at[k], ar.at[k],
                device_id={"section": s, "expert": to, "dp": d}, device_id_type=MESH,
            ).start()
            return carry

        lax.fori_loop(1, EXPERTS, send, 0)
        arecv[k, mine] = asend[k, mine]

    partial(0)
    @pl.when(enters_late == 1)
    def _():
        enter()

    swap(0)
    partial(1)
    swap(1)
    spread_out(0)
    partial(2)
    swap(2)
    partial(3)
    swap(3)
    for k in range(1, HI):
        spread_out(k)

    spread = (iota((ROWSP, EXPERTS), 0) // CAPP == iota((ROWSP, EXPERTS), 1)).astype(F32).astype(BF16)
    pos_f, pos_b = positions(rfv[...]), positions(rbv[...])
    within = (iota((ROWSP, TOKP), 0) % CAPP).astype(F32)
    map_f = (dot(spread, pos_f) == within).astype(F32).astype(BF16)
    within_t = (iota((TOKP, ROWSP), 1) % CAPP).astype(F32)
    same = (iota((TOKP, TOKP), 0) == iota((TOKP, TOKP), 1)).astype(F32).astype(BF16)
    pos_b = dot_t(same, pos_b).astype(BF16)
    map_b = (dot_t(pos_b, spread) == within_t).astype(F32).astype(BF16)

    shift.wait_recv()
    fsend[...] = dot(map_f, trecv[...]).astype(BF16)
    for p in range(PIECES):
        lanes = pl.ds(p * WIDE, WIDE)

        def send_f(i, carry, p=p, lanes=lanes):
            to = plane(i)
            pltpu.make_async_remote_copy(
                fsend.at[pl.ds(pl.multiple_of(to * CAPP, CAPP), CAPP), lanes], frecv.at[mine, lanes], fs.at[p], fr.at[p],
                device_id={"section": s, "expert": to, "dp": d}, device_id_type=MESH,
            ).start()
            return carry

        lax.fori_loop(1, EXPERTS, send_f, 0)
    frecv[mine, :] = fsend[mine, :]

    most = pl.ds(0, ROWSP - CAPP)
    out_z = [
        pltpu.make_async_remote_copy(
            zsend.at[k], zrecv.at[k], zs.at[k], zr.at[k],
            device_id={"section": s, "expert": e, "dp": hi(FAR_FIRST[k]) * 2 + c}, device_id_type=MESH,
        )
        for k in range(HI - 1)
    ]

    def combine(k):
        pltpu.make_async_copy(asend.at[k, most], arecv.at[k, most], ar.at[k]).wait()
        total = dot(map_b, arecv[k])[0:TOK].astype(BF16)
        for j in range(TILES):
            zsend[k, j * TOK : (j + 1) * TOK, :] = total[:, j * LANES : (j + 1) * LANES]
        zsend[k, TILES * TOK : PACK, :] = jnp.zeros((PACK - TILES * TOK, LANES), BF16)

    for k in range(HI - 1):
        combine(k)

        @pl.when(rank(hi(FAR_FIRST[k])) < rank(h))
        def _(k=k):
            out_z[k].start()

    combine(HI - 1)

    for k in (1, 2, 0):

        @pl.when(rank(hi(FAR_FIRST[k])) > rank(h))
        def _(k=k):
            pl.semaphore_wait(ready.at[k], 1)
            out_z[k].start()

    swaps_f = []
    for p in range(PIECES):
        lanes = pl.ds(p * WIDE, WIDE)
        pltpu.make_async_copy(fsend.at[most, lanes], frecv.at[most, lanes], fr.at[p]).wait()
        copy = pltpu.make_async_remote_copy(
            frecv.at[:, lanes], foth.at[:, lanes], gs.at[p], gr.at[p], device_id=other, device_id_type=MESH
        )
        copy.start()
        swaps_f.append(copy)
    near = pl.ds(pl.multiple_of(c * HALF, HALF), HALF)
    far = pl.ds(pl.multiple_of((1 - c) * HALF, HALF), HALF)
    gate = dot_t(frecv[...], gwv[:, near])
    up = dot_t(frecv[...], uwv[:, near])
    for copy in swaps_f:
        copy.wait_recv()
    gate = gate + dot_t(foth[...], gwv[:, far])
    up = up + dot_t(foth[...], uwv[:, far])
    hidden = (gate * jax.nn.sigmoid(gate) * up).astype(BF16)
    hidv[...] = dot(padding((ROWS, ROWSP), 0), hidden).astype(BF16)
    keep = [
        pltpu.make_async_copy(hidv, hidden_ref, out_sem.at[0]),
        pltpu.make_async_copy(zsend.at[HI - 1], zrecv.at[HI - 1], out_sem.at[1]),
    ]
    for copy in keep:
        copy.start()

    for copy in keep:
        copy.wait()
    for copy in out_z:
        copy.wait_recv()
    shift.wait_send()
    for copy in (*swaps, *out_z, *swaps_f):
        copy.wait_send()
    for k in range(HI):
        pltpu.make_async_copy(asend.at[k, most], arecv.at[k, most], as_.at[k]).wait()
    for p in range(PIECES):
        lanes = pl.ds(p * WIDE, WIDE)
        pltpu.make_async_copy(fsend.at[most, lanes], frecv.at[most, lanes], fs.at[p]).wait()


def finish(hidden, blocks, hidden_out, grad_out, hidv, blocksv, gradv, sem):
    fetch = pltpu.make_async_copy(blocks, blocksv, sem.at[0])
    fetch.start()
    bring = pltpu.make_async_copy(hidden, hidv, sem.at[1])
    bring.start()
    fetch.wait()
    total = blocksv[0].astype(F32)
    for k in range(1, HI):
        total = total + blocksv[k].astype(F32)
    total = total.astype(BF16)
    for j in range(TILES):
        gradv[:, j * LANES : (j + 1) * LANES] = total[j * TOK : (j + 1) * TOK]
    out = pltpu.make_async_copy(gradv, grad_out.at[0], sem.at[2])
    out.start()
    bring.wait()
    put = pltpu.make_async_copy(hidv, hidden_out.at[0, 0], sem.at[3])
    put.start()
    out.wait()
    put.wait()


def turned(a):
    return jnp.swapaxes(a, 1, 2)


def per_device(section_out, routes_fwd, gate_weight, up_weight, routes_bwd, saved_gate, saved_up, grad_hidden):
    width = gate_weight.shape[2]
    hbm = pl.BlockSpec(memory_space=pltpu.HBM)
    dma = pltpu.SemaphoreType.DMA
    hidden, blocks = pl.pallas_call(
        kernel,
        out_shape=(
            jax.ShapeDtypeStruct((ROWS, width), BF16),
            jax.ShapeDtypeStruct((HI, PACK, LANES), BF16),
        ),
        in_specs=[hbm] * 8,
        out_specs=(hbm, hbm),
        scratch_shapes=[
            pltpu.VMEM((ROWS, width), BF16),
            pltpu.VMEM((TOK, D), BF16),
            pltpu.VMEM(routes_fwd.shape[:0:-1], jnp.int32),
            pltpu.VMEM(routes_bwd.shape[:0:-1], jnp.int32),
            pltpu.VMEM((width, D), BF16),
            pltpu.VMEM((width, D), BF16),
            pltpu.VMEM((ROWS, width), BF16),
            pltpu.VMEM((ROWS, width), BF16),
            pltpu.VMEM((ROWS, width), BF16),
            pltpu.VMEM((TOKP, HALF), BF16),
            pltpu.VMEM((TOKP, HALF), BF16),
            pltpu.VMEM((HI, 2, ROWSP, BLOCK), BF16),
            pltpu.VMEM((HI, ROWSP, BLOCK), BF16),
            pltpu.VMEM((HI, ROWSP, BLOCK), BF16),
            pltpu.VMEM((HI, ROWSP, BLOCK), BF16),
            pltpu.VMEM((HI, PACK, LANES), BF16),
            pltpu.VMEM((ROWSP, HALF), BF16),
            pltpu.VMEM((ROWSP, HALF), BF16),
            pltpu.VMEM((ROWSP, HALF), BF16),
            dma((2,)), dma((3,)), dma((3,)), dma((HI, 2)), dma, dma, dma((HI,)), dma((HI,)), dma((HI,)), dma((HI,)),
            dma((HI - 1,)), dma((HI - 1,)), dma((PIECES,)), dma((PIECES,)), dma((PIECES,)), dma((PIECES,)),
            pltpu.SemaphoreType.REGULAR((HI - 1,)), pltpu.SemaphoreType.REGULAR,
        ],
        compiler_params=pltpu.CompilerParams(
            collective_id=0, has_side_effects=True, vmem_limit_bytes=60 * 1024 * 1024
        ),
    )(section_out, turned(routes_fwd), turned(gate_weight), turned(up_weight), turned(routes_bwd), saved_gate, saved_up, grad_hidden)
    return pl.pallas_call(
        finish,
        out_shape=(
            jax.ShapeDtypeStruct((1, 1, ROWS, width), BF16),
            jax.ShapeDtypeStruct((1, TOK, BLOCK), BF16),
        ),
        in_specs=[hbm, hbm],
        out_specs=(hbm, hbm),
        scratch_shapes=[
            pltpu.VMEM((ROWS, width), BF16),
            pltpu.VMEM((HI, PACK, LANES), BF16),
            pltpu.VMEM((TOK, BLOCK), BF16),
            dma((4,)),
        ],
        compiler_params=pltpu.CompilerParams(vmem_limit_bytes=60 * 1024 * 1024),
    )(hidden, blocks)


def solution(mesh):
    in_specs = (
        P("section", "expert", None),
        P("section", "expert", None),
        P("expert", None, "dp"),
        P("expert", None, "dp"),
        P("section", "expert", None),
        P("section", "expert", None, "dp"),
        P("section", "expert", None, "dp"),
        P("section", "expert", None, "dp"),
    )
    out_specs = (P("section", "expert", None, "dp"), P("section", "expert", "dp"))
    return jax.shard_map(
        per_device, mesh=mesh, in_specs=in_specs, out_specs=out_specs, check_vma=False
    )
```

```python
import jax
import jax.numpy as jnp
from jax import lax
from jax.experimental import pallas as pl
from jax.experimental.pallas import tpu as pltpu
from jax.sharding import PartitionSpec as P

MESH = pl.DeviceIdType.MESH
F32, BF16 = jnp.float32, jnp.bfloat16

TOK = 40
TOKP = 48
CAP = 13
CAPP = 16
EXPERTS = 16
ROWS = EXPERTS * CAP
ROWSP = EXPERTS * CAPP
D = 3072
HALF = D // 2
BLOCK = D // 8
LANES = 128
TILES = BLOCK // LANES
PACK = 128
HI = 4
PIECES = 3
WIDE = HALF // PIECES
FAR_FIRST = (2, 1, 3, 0)


def dot(a, b):
    return jnp.dot(a, b, preferred_element_type=F32)


def dot_t(a, b):
    return lax.dot_general(a, b, (((1,), (1,)), ((), ())), preferred_element_type=F32)


def iota(shape, dim):
    return lax.broadcasted_iota(jnp.int32, shape, dim)


def positions(routes):
    e = iota((EXPERTS, TOK), 0)
    picked = jnp.zeros((EXPERTS, TOK), F32)
    for k in range(routes.shape[0]):
        picked = picked + (routes[k : k + 1, :] == e).astype(F32)
    picked = picked.astype(BF16)
    row, column = iota((TOK, TOKP), 0), iota((TOK, TOKP), 1)
    earlier = dot(picked, (row < column).astype(F32).astype(BF16))
    here = dot(picked, (row == column).astype(F32).astype(BF16))
    return jnp.where(here > 0.5, earlier, 99.0).astype(BF16)


def padding(shape, slot_dim):
    slot, row = iota(shape, slot_dim), iota(shape, 1 - slot_dim)
    return (slot // CAP * CAPP + slot % CAP == row).astype(F32).astype(BF16)


def kernel(
    sec, rf, gw, uw, rb, sg, su, gh,
    hidden_ref, zrecv,
    hidv, secv, rfv, rbv, gwv, uwv, sgv, suv, ghv,
    tsend, trecv, pbuf, xrecv, asend, arecv, zsend, fsend, frecv, foth,
    out_sem, small_sem, load_sem, w_sem, ts, tr, xs, xr, as_, ar, zs, zr, fs, fr, gs, gr, ready, follows,
):
    s, e, d = lax.axis_index("section"), lax.axis_index("expert"), lax.axis_index("dp")
    h, c = lax.div(d, 2), lax.rem(d, 2)
    other = {"section": s, "expert": e, "dp": h * 2 + (1 - c)}

    def along_z(step):
        z = lax.rem(h * 8 + s + step + 32, 32)
        return {"section": lax.rem(z, 8), "expert": e, "dp": lax.div(z, 8) * 2 + c}

    def plane(i):
        y = lax.rem(lax.div(e, 4) + lax.div(i, 4), 4)
        x = lax.rem(lax.rem(e, 4) + lax.rem(i, 4), 4)
        return y * 4 + x

    def hi(step):
        return lax.rem(h + step, HI)

    def rank(plane_hi):
        return plane_hi + lax.div(plane_hi, 2) * (5 - 2 * plane_hi)

    small = [pltpu.make_async_copy(a.at[0], v, small_sem.at[i]) for i, (a, v) in enumerate(((sec, secv), (rf, rfv), (rb, rbv)))]
    for copy in small:
        copy.start()
    saved = [pltpu.make_async_copy(a.at[0, 0], v, load_sem.at[i]) for i, (a, v) in enumerate(((sg, sgv), (su, suv), (gh, ghv)))]
    for copy in saved:
        copy.start()
    weights = []
    for k in range(HI):
        rows = pl.ds(pl.multiple_of(hi(FAR_FIRST[k]) * 2 * BLOCK, 2 * BLOCK), 2 * BLOCK)
        pair = [
            pltpu.make_async_copy(gw.at[0, :, rows], gwv.at[:, rows], w_sem.at[k, 0]),
            pltpu.make_async_copy(uw.at[0, :, rows], uwv.at[:, rows], w_sem.at[k, 1]),
        ]
        for copy in pair:
            copy.start()
        weights.append((rows, pair))

    barrier = pltpu.get_barrier_semaphore()

    def greet(i, carry):
        pl.semaphore_signal(barrier, inc=1, device_id={"section": s, "expert": plane(i), "dp": d}, device_id_type=MESH)
        return carry

    for step in range(1, HI):

        @pl.when(rank(hi(step)) > rank(h))
        def _(step=step):
            to = {"section": s, "expert": e, "dp": hi(step) * 2 + c}
            pl.semaphore_signal(barrier, inc=1, device_id=to, device_id_type=MESH)

    place = h * 8 + s
    is_last, is_first = lax.div(place, 31), lax.div(31 - place, 31)

    @pl.when(is_first == 0)
    def _():
        pl.semaphore_signal(barrier, inc=1, device_id=along_z(-1), device_id_type=MESH)

    @pl.when(is_last == 1)
    def _():
        pl.semaphore_signal(barrier, inc=1, device_id=along_z(1), device_id_type=MESH)

    pl.semaphore_signal(barrier, inc=1, device_id=other, device_id_type=MESH)
    lax.fori_loop(1, EXPERTS, greet, 0)

    for copy in small:
        copy.wait()

    tsend[0:TOK, :] = secv[:, pl.ds(pl.multiple_of(c * HALF, HALF), HALF)]
    tsend[TOK:TOKP, :] = jnp.zeros((TOKP - TOK, HALF), BF16)

    spread = (iota((ROWSP, EXPERTS), 0) // CAPP == iota((ROWSP, EXPERTS), 1)).astype(F32).astype(BF16)
    pos_f, pos_b = positions(rfv[...]), positions(rbv[...])
    within = (iota((ROWSP, TOKP), 0) % CAPP).astype(F32)
    map_f = (dot(spread, pos_f) == within).astype(F32).astype(BF16)
    within_t = (iota((TOKP, ROWSP), 1) % CAPP).astype(F32)
    same = (iota((TOKP, TOKP), 0) == iota((TOKP, TOKP), 1)).astype(F32).astype(BF16)
    pos_b = dot_t(same, pos_b).astype(BF16)
    map_b = (dot_t(pos_b, spread) == within_t).astype(F32).astype(BF16)

    shift = pltpu.make_async_remote_copy(tsend, trecv, ts, tr, device_id=along_z(1), device_id_type=MESH)

    def enter():
        pl.semaphore_wait(barrier, EXPERTS - 1 + 2 + rank(h) - is_last + is_first)

        @pl.when(is_last == 0)
        def _():
            shift.start()

        @pl.when(is_first == 1)
        def _():
            pl.semaphore_signal(follows, inc=1, device_id=along_z(-1), device_id_type=MESH)

        for k in range(HI - 1):
            lower = hi(HI - FAR_FIRST[k])

            @pl.when(rank(lower) < rank(h))
            def _(k=k, lower=lower):
                to = {"section": s, "expert": e, "dp": lower * 2 + c}
                pl.semaphore_signal(ready.at[k], inc=1, device_id=to, device_id_type=MESH)

    enters_late = lax.div(rank(h), HI - 1) + is_last + is_first

    @pl.when(enters_late == 0)
    def _():
        enter()

    @pl.when(is_last == 1)
    def _():
        pl.semaphore_wait(follows, 1)
        shift.start()

    for copy in saved:
        copy.wait()
    g, u, ct = sgv[...].astype(F32), suv[...].astype(F32), ghv[...].astype(F32)
    sig = jax.nn.sigmoid(g)
    grad_up = (ct * g * sig).astype(BF16)
    grad_gate = (ct * u * sig * (1.0 + g * (1.0 - sig))).astype(BF16)
    pad = padding((ROWSP, ROWS), 1)
    grad_up = dot(pad, grad_up).astype(BF16)
    grad_gate = dot(pad, grad_gate).astype(BF16)
    mine = pl.ds(pl.multiple_of(e * CAPP, CAPP), CAPP)
    swaps = []

    def partial(k):
        rows, pair = weights[k]
        for copy in pair:
            copy.wait()
        part = dot(grad_gate, gwv[:, rows]) + dot(grad_up, uwv[:, rows])
        pbuf[k, 0] = part[:, :BLOCK].astype(BF16)
        pbuf[k, 1] = part[:, BLOCK:].astype(BF16)

    def swap(k):
        copy = pltpu.make_async_remote_copy(
            pbuf.at[k, 1 - c], xrecv.at[k], xs.at[k], xr.at[k], device_id=other, device_id_type=MESH
        )
        copy.start()
        swaps.append(copy)

    def spread_out(k):
        swaps[k].wait_recv()
        asend[k] = (pbuf[k, c].astype(F32) + xrecv[k].astype(F32)).astype(BF16)

        def send(i, carry):
            to = plane(i)
            pltpu.make_async_remote_copy(
                asend.at[k, pl.ds(pl.multiple_of(to * CAPP, CAPP), CAPP)], arecv.at[k, mine], as_.at[k], ar.at[k],
                device_id={"section": s, "expert": to, "dp": d}, device_id_type=MESH,
            ).start()
            return carry

        lax.fori_loop(1, EXPERTS, send, 0)
        arecv[k, mine] = asend[k, mine]

    partial(0)
    @pl.when(enters_late == 1)
    def _():
        enter()

    swap(0)
    partial(1)
    swap(1)
    spread_out(0)
    partial(2)
    swap(2)
    partial(3)
    swap(3)
    for k in range(1, HI):
        spread_out(k)

    shift.wait_recv()
    fsend[...] = dot(map_f, trecv[...]).astype(BF16)
    for p in range(PIECES):
        lanes = pl.ds(p * WIDE, WIDE)

        def send_f(i, carry, p=p, lanes=lanes):
            to = plane(i)
            pltpu.make_async_remote_copy(
                fsend.at[pl.ds(pl.multiple_of(to * CAPP, CAPP), CAPP), lanes], frecv.at[mine, lanes], fs.at[p], fr.at[p],
                device_id={"section": s, "expert": to, "dp": d}, device_id_type=MESH,
            ).start()
            return carry

        lax.fori_loop(1, EXPERTS, send_f, 0)
    frecv[mine, :] = fsend[mine, :]

    most = pl.ds(0, ROWSP - CAPP)
    out_z = [
        pltpu.make_async_remote_copy(
            zsend.at[k], zrecv.at[k], zs.at[k], zr.at[k],
            device_id={"section": s, "expert": e, "dp": hi(FAR_FIRST[k]) * 2 + c}, device_id_type=MESH,
        )
        for k in range(HI - 1)
    ]

    def combine(k):
        pltpu.make_async_copy(asend.at[k, most], arecv.at[k, most], ar.at[k]).wait()
        total = dot(map_b, arecv[k])[0:TOK].astype(BF16)
        for j in range(TILES):
            zsend[k, j * TOK : (j + 1) * TOK, :] = total[:, j * LANES : (j + 1) * LANES]
        zsend[k, TILES * TOK : PACK, :] = jnp.zeros((PACK - TILES * TOK, LANES), BF16)

    for k in range(HI - 1):
        combine(k)

        @pl.when(rank(hi(FAR_FIRST[k])) < rank(h))
        def _(k=k):
            out_z[k].start()

    combine(HI - 1)

    for k in (1, 2, 0):

        @pl.when(rank(hi(FAR_FIRST[k])) > rank(h))
        def _(k=k):
            pl.semaphore_wait(ready.at[k], 1)
            out_z[k].start()

    swaps_f = []
    for p in range(PIECES):
        lanes = pl.ds(p * WIDE, WIDE)
        pltpu.make_async_copy(fsend.at[most, lanes], frecv.at[most, lanes], fr.at[p]).wait()
        copy = pltpu.make_async_remote_copy(
            frecv.at[:, lanes], foth.at[:, lanes], gs.at[p], gr.at[p], device_id=other, device_id_type=MESH
        )
        copy.start()
        swaps_f.append(copy)
    near = pl.ds(pl.multiple_of(c * HALF, HALF), HALF)
    far = pl.ds(pl.multiple_of((1 - c) * HALF, HALF), HALF)
    gate = dot_t(frecv[...], gwv[:, near])
    up = dot_t(frecv[...], uwv[:, near])
    for copy in swaps_f:
        copy.wait_recv()
    gate = gate + dot_t(foth[...], gwv[:, far])
    up = up + dot_t(foth[...], uwv[:, far])
    hidden = (gate * jax.nn.sigmoid(gate) * up).astype(BF16)
    hidv[...] = dot(padding((ROWS, ROWSP), 0), hidden).astype(BF16)
    keep = [
        pltpu.make_async_copy(hidv, hidden_ref, out_sem.at[0]),
        pltpu.make_async_copy(zsend.at[HI - 1], zrecv.at[HI - 1], out_sem.at[1]),
    ]
    for copy in keep:
        copy.start()

    for copy in keep:
        copy.wait()
    for copy in out_z:
        copy.wait_recv()
    shift.wait_send()
    for copy in (*swaps, *out_z, *swaps_f):
        copy.wait_send()
    for k in range(HI):
        pltpu.make_async_copy(asend.at[k, most], arecv.at[k, most], as_.at[k]).wait()
    for p in range(PIECES):
        lanes = pl.ds(p * WIDE, WIDE)
        pltpu.make_async_copy(fsend.at[most, lanes], frecv.at[most, lanes], fs.at[p]).wait()


def finish(hidden, blocks, hidden_out, grad_out, hidv, blocksv, gradv, sem):
    fetch = pltpu.make_async_copy(blocks, blocksv, sem.at[0])
    fetch.start()
    bring = pltpu.make_async_copy(hidden, hidv, sem.at[1])
    bring.start()
    fetch.wait()
    total = blocksv[0].astype(F32)
    for k in range(1, HI):
        total = total + blocksv[k].astype(F32)
    total = total.astype(BF16)
    for j in range(TILES):
        gradv[:, j * LANES : (j + 1) * LANES] = total[j * TOK : (j + 1) * TOK]
    out = pltpu.make_async_copy(gradv, grad_out.at[0], sem.at[2])
    out.start()
    bring.wait()
    put = pltpu.make_async_copy(hidv, hidden_out.at[0, 0], sem.at[3])
    put.start()
    out.wait()
    put.wait()


def turned(a):
    return jnp.swapaxes(a, 1, 2)


def per_device(section_out, routes_fwd, gate_weight, up_weight, routes_bwd, saved_gate, saved_up, grad_hidden):
    width = gate_weight.shape[2]
    hbm = pl.BlockSpec(memory_space=pltpu.HBM)
    dma = pltpu.SemaphoreType.DMA
    hidden, blocks = pl.pallas_call(
        kernel,
        out_shape=(
            jax.ShapeDtypeStruct((ROWS, width), BF16),
            jax.ShapeDtypeStruct((HI, PACK, LANES), BF16),
        ),
        in_specs=[hbm] * 8,
        out_specs=(hbm, hbm),
        scratch_shapes=[
            pltpu.VMEM((ROWS, width), BF16),
            pltpu.VMEM((TOK, D), BF16),
            pltpu.VMEM(routes_fwd.shape[:0:-1], jnp.int32),
            pltpu.VMEM(routes_bwd.shape[:0:-1], jnp.int32),
            pltpu.VMEM((width, D), BF16),
            pltpu.VMEM((width, D), BF16),
            pltpu.VMEM((ROWS, width), BF16),
            pltpu.VMEM((ROWS, width), BF16),
            pltpu.VMEM((ROWS, width), BF16),
            pltpu.VMEM((TOKP, HALF), BF16),
            pltpu.VMEM((TOKP, HALF), BF16),
            pltpu.VMEM((HI, 2, ROWSP, BLOCK), BF16),
            pltpu.VMEM((HI, ROWSP, BLOCK), BF16),
            pltpu.VMEM((HI, ROWSP, BLOCK), BF16),
            pltpu.VMEM((HI, ROWSP, BLOCK), BF16),
            pltpu.VMEM((HI, PACK, LANES), BF16),
            pltpu.VMEM((ROWSP, HALF), BF16),
            pltpu.VMEM((ROWSP, HALF), BF16),
            pltpu.VMEM((ROWSP, HALF), BF16),
            dma((2,)), dma((3,)), dma((3,)), dma((HI, 2)), dma, dma, dma((HI,)), dma((HI,)), dma((HI,)), dma((HI,)),
            dma((HI - 1,)), dma((HI - 1,)), dma((PIECES,)), dma((PIECES,)), dma((PIECES,)), dma((PIECES,)),
            pltpu.SemaphoreType.REGULAR((HI - 1,)), pltpu.SemaphoreType.REGULAR,
        ],
        compiler_params=pltpu.CompilerParams(
            collective_id=0, has_side_effects=True, vmem_limit_bytes=60 * 1024 * 1024
        ),
    )(section_out, turned(routes_fwd), turned(gate_weight), turned(up_weight), turned(routes_bwd), saved_gate, saved_up, grad_hidden)
    return pl.pallas_call(
        finish,
        out_shape=(
            jax.ShapeDtypeStruct((1, 1, ROWS, width), BF16),
            jax.ShapeDtypeStruct((1, TOK, BLOCK), BF16),
        ),
        in_specs=[hbm, hbm],
        out_specs=(hbm, hbm),
        scratch_shapes=[
            pltpu.VMEM((ROWS, width), BF16),
            pltpu.VMEM((HI, PACK, LANES), BF16),
            pltpu.VMEM((TOK, BLOCK), BF16),
            dma((4,)),
        ],
        compiler_params=pltpu.CompilerParams(vmem_limit_bytes=60 * 1024 * 1024),
    )(hidden, blocks)


def solution(mesh):
    in_specs = (
        P("section", "expert", None),
        P("section", "expert", None),
        P("expert", None, "dp"),
        P("expert", None, "dp"),
        P("section", "expert", None),
        P("section", "expert", None, "dp"),
        P("section", "expert", None, "dp"),
        P("section", "expert", None, "dp"),
    )
    out_specs = (P("section", "expert", None, "dp"), P("section", "expert", "dp"))
    return jax.shard_map(
        per_device, mesh=mesh, in_specs=in_specs, out_specs=out_specs, check_vma=False
    )
```
